512 devices in a mesh: patch: 64 (over z, y_lo, core), head: 8 (over y_hi, x).
Axes of the slice: x: 4, y: 8 (y_hi: 2, y_lo: 4; y = y_hi * 4 + y_lo), z: 8, core: 2. Of those that a mesh axis runs over, the one named last changes fastest.
Arguments:
- fresh: bfloat16 [3, 4, 1024, 3072], P(None, None, 'patch', 'head'), may hold values from -18 to 18
- still_masked: int32 [4, 1024], P(None, 'patch'), may hold values 0 or 1
- actions: int32 [4], replicated, may hold values from 0 to 7
- action_table: bfloat16 [8, 3, 3072], P(None, None, 'head'), may hold values from -3 to 3
- mask_vector: bfloat16 [3, 3072], P(None, 'head'), may hold values from -4 to 4
- position: bfloat16 [3, 1024, 3072], P(None, 'patch', 'head'), may hold values from -4 to 4
- cache: bfloat16 [2, 16, 4, 1024, 3072], P(None, None, None, 'patch', 'head'), may hold values from -18 to 18
- w_out: bfloat16 [3072, 5120], P('head', 'patch'), may hold values from -0.109375 to 0.109375
Outputs:
- update: float32 [4, 1024, 5120], P(None, 'patch', 'head')
The draws below stay inside these ranges and needn't reach their ends.
All inputs are finite; a program needn't handle non-finite values. No bound on the sum of `still_masked` on one device may be relied on, other than what follows from the above.
Results may differ from the reference program's by a relative error of at most 0.0082.
Values may be sent and summed in bfloat16 or wider, within the bound.
A program may use at most 64 MiB of HBM per device.

```python
import jax
import jax.numpy as jnp
from jax import lax

D = 5120
HD = 128
HEADS = 24
NACT = 8
ROLL = 4
FRAMES = 16
HW = 3072
PATCHES = 1024


def draw_fresh(key, part):
    key = jax.random.fold_in(key, 11)
    out = jax.random.truncated_normal(key, -4.0, 4.0, (3, ROLL, PATCHES, HW), jnp.float32)
    return out.astype(jnp.bfloat16)


def draw_position(key, part):
    key = jax.random.fold_in(key, 37)
    out = jax.random.truncated_normal(key, -4.0, 4.0, (3, PATCHES, HW), jnp.float32)
    return out.astype(jnp.bfloat16)


def draw_cache(key, part):
    key = jax.random.fold_in(key, 23)
    out = jax.random.truncated_normal(key, -4.0, 4.0, (2, FRAMES, ROLL, PATCHES, HW), jnp.float32)
    return out.astype(jnp.bfloat16)


def place_ends(values, own_key, least, top_value):
    index_at = [jax.random.randint(jax.random.fold_in(own_key, axis), (), 0, length) for axis, length in enumerate(values.shape)]
    longest = values.shape.index(max(values.shape))
    neighbour = index_at[:longest] + [(index_at[longest] + 1) % values.shape[longest]] + index_at[longest + 1:]
    return values.at[tuple(index_at)].set(least).at[tuple(neighbour)].set(top_value)


def steps_of(rng, dims, split, least, high):
    def one(dim, shards_of):
        draws = jax.random.uniform(jax.random.fold_in(jax.random.fold_in(rng, 6), dim), (shards_of,), jnp.float32, least / len(split), high / len(split))
        return jnp.repeat(jnp.exp(draws), dims[dim] // shards_of).reshape((-1,) + (1,) * (len(dims) - dim - 1))

    loudness = one(*split[0])
    for cut in split[1:]:
        loudness = loudness * one(*cut)
    return loudness


def bell_draw(stream_key, dims, deviation, limit, pieces=(), kind=jnp.bfloat16):
    entries = jax.random.normal(stream_key, dims, jnp.float32) * deviation
    if len(pieces) > 0:
        entries = steps_of(stream_key, dims, pieces, -0.22, 0.18) * entries
    return jnp.clip(entries, min=-limit, max=limit).astype(kind)


def setup_inputs(seed: int = 0) -> dict:
    key_of = jax.random.split(jax.random.key(seed), 9)
    fresh = draw_fresh(jax.random.fold_in(key_of[8], 71), 0)
    still_masked = place_ends((jax.random.randint(key_of[1], (ROLL, PATCHES), 0, 2) < 1).astype(jnp.int32), jax.random.fold_in(key_of[1], 1), 0, 1)
    actions = place_ends(jax.random.randint(key_of[2], (ROLL,), 0, NACT), jax.random.fold_in(key_of[2], 1), 0, NACT - 1).astype(jnp.int32)
    action_table = bell_draw(key_of[3], (NACT, 3, HW), 0.5, 3.0, ((2, 8),))
    mask_vector = bell_draw(key_of[4], (3, HW), 1.0, 4.0, ((1, 8),))
    position = draw_position(jax.random.fold_in(key_of[8], 71), 0)
    cache = draw_cache(jax.random.fold_in(key_of[8], 71), 0)
    w_out = bell_draw(key_of[7], (HW, D), HW ** -0.5, 0.109375, ((0, 8), (1, 64)))
    return dict(fresh=fresh, still_masked=still_masked, actions=actions, action_table=action_table, mask_vector=mask_vector, position=position, cache=cache, w_out=w_out)


def reference(fresh, still_masked, actions, action_table, mask_vector, position, cache, w_out):
    onehot = (actions[:, None] == jnp.arange(NACT, dtype=jnp.int32)[None, :]).astype(jnp.float32)
    bias = jnp.einsum('ra,ach->crh', onehot, action_table.astype(jnp.float32))
    base = jnp.where(still_masked[None, :, :, None] == 1, mask_vector.astype(jnp.float32)[:, None, None, :], fresh.astype(jnp.float32))
    embed = (base + bias[:, :, None, :] + position.astype(jnp.float32)[:, None, :, :]).astype(jnp.bfloat16)
    scale = HD ** -0.5

    def by_head(x):
        return jnp.moveaxis(x.reshape(x.shape[:-1] + (HEADS, HD)), -2, 0)

    query = by_head(embed[0])
    key = by_head(embed[1])
    value = by_head(embed[2])
    cache_key = by_head(cache[0])
    cache_value = by_head(cache[1])

    def one_head(items):
        q, k, v, ck, cv = items
        qf = q.astype(jnp.float32)
        vf = v.astype(jnp.float32)
        s = jnp.einsum('rpd,rkd->rpk', qf, k.astype(jnp.float32)) * scale
        m = jnp.max(s, axis=-1, keepdims=True)
        e = jnp.exp(s - m)
        total = jnp.sum(e, axis=-1, keepdims=True)
        w = e.astype(jnp.bfloat16).astype(jnp.float32)
        spatial = jnp.einsum('rpk,rkd->rpd', w, vf) / total
        ts = jnp.einsum('rpd,frpd->frp', qf, ck.astype(jnp.float32)) * scale
        own = jnp.sum(qf * k.astype(jnp.float32), axis=-1) * scale
        tm = jnp.maximum(jnp.max(ts, axis=0), own)
        te = jnp.exp(ts - tm[None])
        oe = jnp.exp(own - tm)
        ttotal = jnp.sum(te, axis=0) + oe
        tw = te.astype(jnp.bfloat16).astype(jnp.float32)
        ow = oe.astype(jnp.bfloat16).astype(jnp.float32)
        temporal = (jnp.einsum('frp,frpd->rpd', tw, cv.astype(jnp.float32)) + ow[..., None] * vf) / ttotal[..., None]
        return spatial + temporal

    mixed = lax.map(one_head, (query, key, value, cache_key, cache_value))
    attended = jnp.moveaxis(mixed, 0, -2).reshape(ROLL, PATCHES, HW).astype(jnp.bfloat16)
    update = jnp.dot(attended.reshape(ROLL * PATCHES, HW), w_out, preferred_element_type=jnp.float32)
    return update.reshape(ROLL, PATCHES, D)
```

```python
import functools

import jax
import jax.numpy as jnp
from jax import lax
from jax.experimental import pallas as pl
from jax.experimental.pallas import tpu as pltpu
from jax.sharding import PartitionSpec as P

HD = 128
NACT = 8
ROLL = 4
FRAMES = 16
SCALE = HD ** (-0.5)
LOG2E = 1.4426950408889634
PLACE = (0, 3, 5)
ZROWS, YROWS = 48, 32
NROWS = ZROWS + YROWS

BF16, F32 = jnp.bfloat16, jnp.float32


def nt_dot(a, b):
    return lax.dot_general(a, b, (((1,), (1,)), ((), ())), preferred_element_type=F32)


def kernel(
    actions, still_ref, table_ref, maskv_ref, fresh_hbm, pos_hbm, cache_hbm, w_hbm, out_ref,
    fresh, pos, cache, w_own, emb, qkv, kv_peer, o_buf, spat, temp, zg, yg, b_buf,
    cx_send, cx_own, cx_recv, y_send, y_recv,
    in_sem, qkv_sem, kv_sem, o_sem, t_sem, zg_sem, yg_sem, b_sem, bc_sem, cx_sem, y_sem,
    qkv_out, kv_out, o_out, t_out, zg_out, yg_out, bz_out, by_out, bc_out, cx_out, y_out,
):
    patch, head = lax.axis_index("patch"), lax.axis_index("head")
    z, yl, c = patch // 8, (patch // 2) % 4, patch % 2
    yh, x = head // 4, head % 4
    half = (z + yl) % 2
    base = (z // 2) * 2

    def at(z_=None, yl_=None, c_=None, yh_=None, x_=None):
        z_, yl_ = z if z_ is None else z_, yl if yl_ is None else yl_
        c_, yh_ = c if c_ is None else c_, yh if yh_ is None else yh_
        x_ = x if x_ is None else x_
        return {"patch": z_ * 8 + yl_ * 2 + c_, "head": yh_ * 4 + x_}

    def remote(src, dst, send, recv, device):
        return pltpu.make_async_remote_copy(
            src_ref=src, dst_ref=dst, send_sem=send, recv_sem=recv,
            device_id=device, device_id_type=pl.DeviceIdType.MESH,
        )

    def await_bytes(ref, sem):
        pltpu.make_async_copy(ref, ref, sem).wait()

    barrier = pltpu.get_barrier_semaphore()

    def hail(device):
        pl.semaphore_signal(barrier, inc=1, device_id=device, device_id_type=pl.DeviceIdType.MESH)

    def hail_group(i, carry):
        s = (z * 4 + yl + i) % 32
        hail(at(z_=s // 4, yl_=s % 4))
        return carry

    lax.fori_loop(1, 32, hail_group, 0)
    hail(at(c_=1 - c))
    for k in (1, 2, 3):
        hail(at(x_=(x + k) % 4))
    hail(at(yh_=1 - yh))
    hail(at(yh_=1 - yh, z_=base + 1 - z % 2))

    loads = [
        pltpu.make_async_copy(src, dst, in_sem.at[i])
        for i, (src, dst) in enumerate(
            ((fresh_hbm, fresh), (pos_hbm, pos), (w_hbm, w_own), (cache_hbm, cache))
        )
    ]
    for load in loads:
        load.start()

    loads[0].wait()
    loads[1].wait()
    diagonal = lax.broadcasted_iota(jnp.int32, (16, 16), 0) == lax.broadcasted_iota(
        jnp.int32, (16, 16), 1
    )
    row_of = lax.broadcasted_iota(jnp.int32, (NACT, 384), 0)
    for r in range(ROLL):
        flags = jnp.broadcast_to(still_ref[r : r + 1, :], (16, 16))
        masked = jnp.sum(jnp.where(diagonal, flags, 0).astype(F32), axis=1, keepdims=True) > 0.5
        for i in range(3):
            bias = jnp.sum(
                jnp.where(row_of == actions[r], table_ref[i].astype(F32), 0.0), axis=0, keepdims=True
            )
            mask_row = maskv_ref[i : i + 1, :].astype(F32)
            start = jnp.where(masked, mask_row, fresh[i, r].astype(F32))
            whole = (start + bias + pos[i].astype(F32)).astype(BF16)
            for h in range(3):
                emb[r * 3 + h, i] = whole[:, h * HD : (h + 1) * HD]

    loads[3].wait()

    def temporal(r, carry):
        for h in range(3):
            lanes = slice(h * HD, (h + 1) * HD)
            q = emb[r * 3 + h, 0].astype(F32)
            own_k = emb[r * 3 + h, 1].astype(F32)
            own_v = emb[r * 3 + h, 2].astype(F32)
            keys = cache[0, :, r, :, lanes].astype(F32)
            s = jnp.sum(q[None] * keys, axis=-1, keepdims=True) * SCALE
            own = jnp.sum(q * own_k, axis=-1, keepdims=True) * SCALE
            peak = jnp.maximum(jnp.max(s, axis=0), own)
            e = jnp.exp(s - peak[None])
            own_e = jnp.exp(own - peak)
            total = jnp.sum(e, axis=0) + own_e
            weights = e.astype(BF16).astype(F32)
            values = cache[1, :, r, :, lanes].astype(F32)
            summed = jnp.sum(weights * values, axis=0)
            summed = summed + own_e.astype(BF16).astype(F32) * own_v
            temp[z % 2, r, :, lanes] = summed / total
        return carry

    lax.fori_loop(0, ROLL, temporal, 0)

    loads[2].wait()
    pl.semaphore_wait(barrier, 37)

    me = z * 4 + yl
    pair_head = jnp.int32(-1)
    for h in range(3):
        pair_head = jnp.where((2 * yl + PLACE[h]) % 8 == z, h, pair_head)
    attends = pair_head >= 0
    for r in range(ROLL):
        for h in range(3):
            zd = (2 * r + PLACE[h]) % 8
            here = jnp.logical_and(z == zd, yl == r)

            @pl.when(here)
            def _(r=r, h=h):
                pltpu.make_async_copy(emb.at[r * 3 + h], qkv.at[me], qkv_sem).start()

            @pl.when(jnp.logical_not(here))
            def _(r=r, h=h, zd=zd):
                remote(
                    emb.at[r * 3 + h], qkv.at[me], qkv_out, qkv_sem, at(z_=zd, yl_=r)
                ).start()

    pltpu.make_async_copy(w_own.at[pl.ds(ZROWS, YROWS)], yg.at[yl], yg_sem).start()
    for k in range(1, 4):
        remote(
            w_own.at[pl.ds(ZROWS, YROWS)], yg.at[yl], yg_out, yg_sem, at(yl_=(yl + k) % 4)
        ).start()
    pltpu.make_async_copy(w_own.at[pl.ds(0, ZROWS)], zg.at[z], zg_sem).start()
    for k in range(1, 8):
        remote(
            w_own.at[pl.ds(0, ZROWS)], zg.at[z], zg_out, zg_sem, at(z_=(z + k) % 8)
        ).start()
    remote(temp.at[z % 2], temp.at[z % 2], t_out, t_sem, at(z_=base + 1 - z % 2)).start()

    await_bytes(yg, yg_sem)
    first = (z // 4 + yl) % 2

    def spread_z(k, carry):
        zd = first + 2 * k

        @pl.when(zd == z)
        def _():
            pltpu.make_async_copy(
                yg, b_buf.at[z % 4, :, c, pl.ds(ZROWS, YROWS)], b_sem
            ).start()

        @pl.when(zd != z)
        def _():
            remote(
                yg, b_buf.at[z % 4, :, c, pl.ds(ZROWS, YROWS)], by_out, b_sem, at(z_=zd)
            ).start()

        return carry

    lax.fori_loop(0, 4, spread_z, 0)

    @pl.when(attends)
    def _():
        await_bytes(qkv, qkv_sem)
        remote(qkv.at[:, pl.ds(1, 2)], kv_peer, kv_out, kv_sem, at(c_=1 - c)).start()

    await_bytes(zg, zg_sem)
    pltpu.make_async_copy(
        zg.at[pl.ds(half * 4, 4)], b_buf.at[:, yl, c, pl.ds(0, ZROWS)], b_sem
    ).start()
    for k in range(1, 4):
        yd = (yl + k) % 4
        remote(
            zg.at[pl.ds(((z + yd) % 2) * 4, 4)],
            b_buf.at[:, yl, c, pl.ds(0, ZROWS)],
            bz_out, b_sem, at(yl_=yd),
        ).start()

    @pl.when(attends)
    def _():
        await_bytes(kv_peer, kv_sem)
        c2 = SCALE * LOG2E

        def attend(i, carry):
            q = qkv[pl.ds(i * 8, 8), 0].reshape(128, HD)
            s_a = nt_dot(q, qkv[:, 1].reshape(512, HD))
            s_b = nt_dot(q, kv_peer[:, 0].reshape(512, HD))
            peak = jnp.maximum(
                jnp.max(s_a, axis=-1, keepdims=True), jnp.max(s_b, axis=-1, keepdims=True)
            )
            e_a = jnp.exp2((s_a - peak) * c2)
            e_b = jnp.exp2((s_b - peak) * c2)
            total = jnp.sum(e_a, axis=-1, keepdims=True) + jnp.sum(e_b, axis=-1, keepdims=True)
            o = jnp.dot(
                e_a.astype(BF16), qkv[:, 2].reshape(512, HD), preferred_element_type=F32
            ) + jnp.dot(
                e_b.astype(BF16), kv_peer[:, 1].reshape(512, HD), preferred_element_type=F32
            )
            o_buf[i] = (o / total).astype(BF16).reshape(2, 4, 16, HD)
            for b in range(2):
                for yd in range(4):
                    zd = 2 * i + b
                    here = jnp.logical_and(zd == z, yl == yd)
                    src, dst = o_buf.at[i, :, yd], spat.at[pair_head, :, yl]

                    @pl.when(here)
                    def _(src=src, dst=dst):
                        pltpu.make_async_copy(src, dst, o_sem).start()

                    @pl.when(jnp.logical_not(here))
                    def _(src=src, dst=dst, zd=zd, yd=yd):
                        remote(src, dst, o_out, o_sem, at(z_=zd, yl_=yd)).start()

            return carry

        lax.fori_loop(0, 4, attend, 0)

    await_bytes(b_buf.at[:, :, c], b_sem)
    remote(b_buf.at[:, :, c], b_buf.at[:, :, c], bc_out, bc_sem, at(c_=1 - c)).start()

    await_bytes(temp.at[0], t_sem)
    await_bytes(spat, o_sem)
    attended = jnp.concatenate(
        [
            (
                spat[h].astype(F32).reshape(128, HD)
                + temp[:, :, :, h * HD : (h + 1) * HD].reshape(128, HD)
            ).astype(BF16)
            for h in range(3)
        ],
        axis=1,
    )
    await_bytes(b_buf.at[:, :, 1 - c], bc_sem)

    for n, k in enumerate((2, 1, 3)):
        xd = (x + k) % 4
        part = nt_dot(attended, b_buf[xd].reshape(640, 384))
        cx_send[n] = part.astype(BF16).reshape(2, 64, 640)
        remote(
            cx_send.at[n], cx_recv.at[n], cx_out, cx_sem, at(x_=xd)
        ).start()
    cx_own[...] = nt_dot(attended, b_buf[x].reshape(640, 384)).reshape(2, 64, 640)
    await_bytes(cx_recv, cx_sem)

    mine = yh == half

    def total_of(zz):
        return (
            cx_own[zz]
            + cx_recv[0, zz].astype(F32)
            + cx_recv[1, zz].astype(F32)
            + cx_recv[2, zz].astype(F32)
        )

    other = 1 - z % 2
    y_send[0] = total_of(other).astype(BF16)
    remote(
        y_send.at[0], y_recv.at[yh], y_out, y_sem, at(z_=base + other, yh_=half)
    ).start()

    @pl.when(mine)
    def _():
        kept = total_of(z % 2)
        await_bytes(y_recv.at[0], y_sem)
        out_ref[...] = (kept + y_recv[1 - yh].astype(F32)).reshape(4, 16, 640)
        await_bytes(y_send.at[0], y_out)

    @pl.when(jnp.logical_not(mine))
    def _():
        y_send[1] = total_of(z % 2).astype(BF16)
        remote(y_send.at[1], y_recv.at[yh], y_out, y_sem, at(yh_=half)).start()
        await_bytes(y_recv, y_sem)
        out_ref[...] = (y_recv[0].astype(F32) + y_recv[1].astype(F32)).reshape(4, 16, 640)
        await_bytes(y_send, y_out)

    @pl.when(attends)
    def _():
        await_bytes(emb.at[pl.ds(0, 11)], qkv_out)
        await_bytes(kv_peer, kv_out)
        await_bytes(kv_peer.at[pl.ds(0, 31)], o_out)

    @pl.when(jnp.logical_not(attends))
    def _():
        await_bytes(emb, qkv_out)

    await_bytes(yg.at[pl.ds(0, 3)], yg_out)
    await_bytes(zg.at[pl.ds(0, 7)], zg_out)
    await_bytes(temp.at[0], t_out)
    sends = z % 2 == first

    @pl.when(sends)
    def _():
        await_bytes(b_buf.at[pl.ds(0, 3), :, 0, pl.ds(0, YROWS)], by_out)

    @pl.when(jnp.logical_not(sends))
    def _():
        await_bytes(b_buf.at[:, :, 0, pl.ds(0, YROWS)], by_out)

    await_bytes(b_buf.at[:, pl.ds(0, 3), 0, pl.ds(0, ZROWS)], bz_out)
    await_bytes(b_buf.at[:, :, 0], bc_out)
    await_bytes(cx_send, cx_out)


def shards(fresh, still_masked, actions, action_table, mask_vector, position, cache, w_out):
    anywhere = pl.BlockSpec(memory_space=pl.ANY)
    vmem = pl.BlockSpec(memory_space=pltpu.VMEM)
    smem = pl.BlockSpec(memory_space=pltpu.SMEM)
    dma = pltpu.SemaphoreType.DMA
    return pl.pallas_call(
        kernel,
        out_shape=jax.ShapeDtypeStruct((4, 16, 640), F32),
        in_specs=[smem, vmem, vmem, vmem, anywhere, anywhere, anywhere, anywhere],
        out_specs=vmem,
        scratch_shapes=[
            pltpu.VMEM((3, 4, 16, 384), BF16),
            pltpu.VMEM((3, 16, 384), BF16),
            pltpu.VMEM((2, 16, 4, 16, 384), BF16),
            pltpu.VMEM((NROWS, 384), BF16),
            pltpu.VMEM((12, 3, 16, HD), BF16),
            pltpu.VMEM((32, 3, 16, HD), BF16),
            pltpu.VMEM((32, 2, 16, HD), BF16),
            pltpu.VMEM((4, 2, 4, 16, HD), BF16),
            pltpu.VMEM((3, 2, 4, 16, HD), BF16),
            pltpu.VMEM((2, 4, 16, 384), F32),
            pltpu.VMEM((8, ZROWS, 384), BF16),
            pltpu.VMEM((4, YROWS, 384), BF16),
            pltpu.VMEM((4, 4, 2, NROWS, 384), BF16),
            pltpu.VMEM((3, 2, 64, 640), BF16),
            pltpu.VMEM((2, 64, 640), F32),
            pltpu.VMEM((3, 2, 64, 640), BF16),
            pltpu.VMEM((2, 64, 640), BF16),
            pltpu.VMEM((2, 64, 640), BF16),
            dma((4,)),
        ]
        + [dma] * 21,
        compiler_params=pltpu.CompilerParams(
            collective_id=0, has_side_effects=True, vmem_limit_bytes=40 << 20
        ),
        cost_estimate=pl.CostEstimate(
            flops=400_000_000, bytes_accessed=2_000_000, transcendentals=600_000
        ),
    )(
        actions,
        still_masked,
        jnp.transpose(action_table, (1, 0, 2)),
        mask_vector,
        fresh,
        position,
        cache,
        jnp.transpose(w_out),
    )


def solution(mesh):
    placed = (
        P(None, None, "patch", "head"),
        P(None, "patch"),
        P(),
        P(None, None, "head"),
        P(None, "head"),
        P(None, "patch", "head"),
        P(None, None, None, "patch", "head"),
        P("head", "patch"),
    )
    return jax.shard_map(
        shards, mesh=mesh, in_specs=placed, out_specs=P(None, "patch", "head"), check_vma=False
    )
```

```python
import functools

import jax
import jax.numpy as jnp
from jax import lax
from jax.experimental import pallas as pl
from jax.experimental.pallas import tpu as pltpu
from jax.sharding import PartitionSpec as P

HD = 128
NACT = 8
ROLL = 4
FRAMES = 16
SCALE = HD ** (-0.5)
LOG2E = 1.4426950408889634
PLACE = (0, 3, 5)
ZROWS, YROWS = 32, 48
NROWS = ZROWS + YROWS

BF16, F32 = jnp.bfloat16, jnp.float32


def nt_dot(a, b):
    return lax.dot_general(a, b, (((1,), (1,)), ((), ())), preferred_element_type=F32)


def kernel(
    actions, still_ref, table_ref, maskv_ref, fresh_hbm, pos_hbm, cache_hbm, w_hbm, y_out_ref,
    fresh, pos, cache, w_own, emb, qkv, kv_peer, t_send, t_recv, o_buf, att, near, b_buf,
    cx_send, cx_own, cx_recv, y_send,
    in_sem, o_out, cx_sem, qkv_sem, kv_sem, o_sem, t_sem, near_sem, b_sem, bz_sem, by_sem,
    bc_sem, bd_sem, y_sem,
    qkv_out, kv_out, t_out, near_out, b_out, bz_out, by_out, bc_out, bd_out, cx_out, y_out,
):
    patch, head = lax.axis_index("patch"), lax.axis_index("head")
    z, yl, c = patch // 8, (patch // 2) % 4, patch % 2
    yh, x = head // 4, head % 4
    yy, yb = yl // 2, yl % 2
    half = (z + yy) % 2
    base = (z // 2) * 2

    def at(z_=None, yl_=None, c_=None, yh_=None, x_=None):
        z_, yl_ = z if z_ is None else z_, yl if yl_ is None else yl_
        c_, yh_ = c if c_ is None else c_, yh if yh_ is None else yh_
        x_ = x if x_ is None else x_
        return {"patch": z_ * 8 + yl_ * 2 + c_, "head": yh_ * 4 + x_}

    def remote(src, dst, send, recv, device):
        return pltpu.make_async_remote_copy(
            src_ref=src, dst_ref=dst, send_sem=send, recv_sem=recv,
            device_id=device, device_id_type=pl.DeviceIdType.MESH,
        )

    def await_bytes(ref, sem):
        pltpu.make_async_copy(ref, ref, sem).wait()

    loads = [
        pltpu.make_async_copy(src, dst, in_sem.at[i])
        for i, (src, dst) in enumerate(
            ((fresh_hbm, fresh), (pos_hbm, pos), (w_hbm, w_own), (cache_hbm, cache))
        )
    ]
    for load in loads:
        load.start()

    barrier = pltpu.get_barrier_semaphore()

    def hail(device):
        pl.semaphore_signal(barrier, inc=1, device_id=device, device_id_type=pl.DeviceIdType.MESH)

    def hail_group(i, carry):
        s = (z * 4 + yl + i) % 32
        hail(at(z_=s // 4, yl_=s % 4))
        return carry

    lax.fori_loop(1, 32, hail_group, 0)
    hail(at(c_=1 - c))
    for k in (1, 2, 3):
        hail(at(x_=(x + k) % 4))
    for zz in range(2):
        for w in range(2):
            hail(at(yh_=1 - yh, z_=base + zz, yl_=2 * w + yb))

    loads[0].wait()
    loads[1].wait()
    diagonal = lax.broadcasted_iota(jnp.int32, (16, 16), 0) == lax.broadcasted_iota(
        jnp.int32, (16, 16), 1
    )
    row_of = lax.broadcasted_iota(jnp.int32, (NACT, 384), 0)
    for r in range(ROLL):
        flags = jnp.broadcast_to(still_ref[r : r + 1, :], (16, 16))
        masked = jnp.sum(jnp.where(diagonal, flags, 0).astype(F32), axis=1, keepdims=True) > 0.5
        for i in range(3):
            bias = jnp.sum(
                jnp.where(row_of == actions[r], table_ref[i].astype(F32), 0.0), axis=0, keepdims=True
            )
            mask_row = maskv_ref[i : i + 1, :].astype(F32)
            start = jnp.where(masked, mask_row, fresh[i, r].astype(F32))
            whole = (start + bias + pos[i].astype(F32)).astype(BF16)
            for h in range(3):
                emb[r * 3 + h, i] = whole[:, h * HD : (h + 1) * HD]

    loads[2].wait()
    pl.semaphore_wait(barrier, 39)

    me = z * 4 + yl
    pair_head = jnp.int32(-1)
    for h in range(3):
        pair_head = jnp.where((2 * yl + PLACE[h]) % 8 == z, h, pair_head)
    attends = pair_head >= 0

    def to_attending(src, dst, send, recv, r, h):
        zd = (2 * r + PLACE[h]) % 8
        here = jnp.logical_and(z == zd, yl == r)

        @pl.when(here)
        def _():
            pltpu.make_async_copy(src, dst, recv).start()

        @pl.when(jnp.logical_not(here))
        def _():
            remote(src, dst, send, recv, at(z_=zd, yl_=r)).start()

    for r in range(ROLL):
        for h in range(3):
            to_attending(emb.at[r * 3 + h], qkv.at[me], qkv_out, qkv_sem, r, h)

    first = (z // 4 + yy) % 2
    own_rows = pl.multiple_of((yb * 2 + c) * NROWS, 16)
    near_rows = pl.multiple_of(((1 - yb) * 2 + c) * NROWS, 16)

    def spread(src, rows, size, send, recv):
        def one(k, carry):
            zd = first + 2 * k
            dst = b_buf.at[z % 4, pl.ds(rows, size)]

            @pl.when(zd == z)
            def _():
                pltpu.make_async_copy(src, dst, recv).start()

            @pl.when(zd != z)
            def _():
                remote(src, dst, send, recv, at(z_=zd)).start()

            return carry

        lax.fori_loop(0, 4, one, 0)

    remote(
        w_own.at[pl.ds(ZROWS, YROWS)], near, near_out, near_sem, at(yl_=2 * yy + 1 - yb)
    ).start()
    spread(w_own, own_rows, NROWS, b_out, b_sem)

    loads[3].wait()

    def temporal(r, carry):
        for h in range(3):
            lanes = slice(h * HD, (h + 1) * HD)
            q = emb[r * 3 + h, 0].astype(F32)
            own_k = emb[r * 3 + h, 1].astype(F32)
            own_v = emb[r * 3 + h, 2].astype(F32)
            keys = cache[0, :, r, :, lanes].astype(F32)
            s = jnp.sum(q[None] * keys, axis=-1, keepdims=True) * SCALE
            own = jnp.sum(q * own_k, axis=-1, keepdims=True) * SCALE
            peak = jnp.maximum(jnp.max(s, axis=0), own)
            e = jnp.exp(s - peak[None])
            own_e = jnp.exp(own - peak)
            total = jnp.sum(e, axis=0) + own_e
            weights = e.astype(BF16).astype(F32)
            values = cache[1, :, r, :, lanes].astype(F32)
            summed = jnp.sum(weights * values, axis=0)
            summed = summed + own_e.astype(BF16).astype(F32) * own_v
            t_send[r * 3 + h] = (summed / total).astype(BF16)
        return carry

    lax.fori_loop(0, ROLL, temporal, 0)

    for r in range(ROLL):
        for h in range(3):
            to_attending(t_send.at[r * 3 + h], t_recv.at[me], t_out, t_sem, r, h)

    await_bytes(near, near_sem)
    spread(near, near_rows + ZROWS, YROWS, bz_out, bz_sem)

    @pl.when(attends)
    def _():
        await_bytes(qkv, qkv_sem)
        remote(qkv.at[:, pl.ds(1, 2)], kv_peer, kv_out, kv_sem, at(c_=1 - c)).start()

    await_bytes(b_buf.at[:, pl.ds(own_rows, NROWS)], b_sem)
    went = b_buf.at[:, pl.ds(own_rows, ZROWS)]
    remote(went, went, by_out, by_sem, at(yl_=2 * yy + 1 - yb)).start()
    gathered = b_buf.at[:, pl.ds(own_rows, NROWS)]
    remote(gathered, gathered, bc_out, bc_sem, at(c_=1 - c)).start()

    @pl.when(attends)
    def _():
        await_bytes(kv_peer, kv_sem)
        await_bytes(t_recv, t_sem)
        c2 = SCALE * LOG2E

        def attend(i, carry):
            q = qkv[pl.ds(i * 8, 8), 0].reshape(128, HD)
            s_a = nt_dot(q, qkv[:, 1].reshape(512, HD))
            s_b = nt_dot(q, kv_peer[:, 0].reshape(512, HD))
            peak = jnp.maximum(
                jnp.max(s_a, axis=-1, keepdims=True), jnp.max(s_b, axis=-1, keepdims=True)
            )
            e_a = jnp.exp2((s_a - peak) * c2)
            e_b = jnp.exp2((s_b - peak) * c2)
            total = jnp.sum(e_a, axis=-1, keepdims=True) + jnp.sum(e_b, axis=-1, keepdims=True)
            o = jnp.dot(
                e_a.astype(BF16), qkv[:, 2].reshape(512, HD), preferred_element_type=F32
            ) + jnp.dot(
                e_b.astype(BF16), kv_peer[:, 1].reshape(512, HD), preferred_element_type=F32
            )
            o = o / total + t_recv[pl.ds(i * 8, 8)].astype(F32).reshape(128, HD)
            o_buf[i] = o.astype(BF16).reshape(2, 2, 2, 16, HD)
            for b in range(2):
                for yd in range(4):
                    zd = 2 * i + b
                    here = jnp.logical_and(zd == z, yl == yd)
                    src, dst = o_buf.at[i, :, :, yd % 2], att.at[pair_head, :, :, yl]

                    @pl.when(here)
                    def _(src=src, dst=dst):
                        pltpu.make_async_copy(src, dst, o_sem).start()

                    @pl.when(jnp.logical_not(here))
                    def _(src=src, dst=dst, zd=zd, yd=yd):
                        remote(src, dst, o_out.at[i], o_sem, at(z_=zd, yl_=yd)).start()

            return carry

        lax.fori_loop(0, 4, attend, 0)

    await_bytes(b_buf.at[:, pl.ds(near_rows, ZROWS)], by_sem)
    await_bytes(b_buf.at[:, pl.ds(near_rows, YROWS)], bz_sem)
    gathered_near = b_buf.at[:, pl.ds(near_rows, NROWS)]
    remote(gathered_near, gathered_near, bd_out, bd_sem, at(c_=1 - c)).start()

    await_bytes(att, o_sem)
    tokens = [
        jnp.concatenate([att[h, zz].reshape(128, HD) for h in range(3)], axis=1) for zz in range(2)
    ]
    stacked = jnp.concatenate(tokens, axis=0)
    beside = jnp.concatenate(tokens, axis=1)
    blank = jnp.zeros((64, 384), BF16)
    main_rows = pl.multiple_of(yy * 64, 64)
    tail_rows = pl.multiple_of((1 - yy) * 256, 64)
    mine = yh == half
    early = jnp.where(mine, 1 - yy, yy)
    order = (early, 1 - early)
    await_bytes(b_buf.at[:, pl.ds(own_rows, NROWS)], bc_sem)
    await_bytes(b_buf.at[:, pl.ds(near_rows, NROWS)], bd_sem)

    def project(xd):
        main = nt_dot(stacked, b_buf[xd, pl.ds(main_rows, 256), :]).reshape(2, 2, 64, 256)
        ends = b_buf[xd, pl.ds(tail_rows, 64), :]
        weights = jnp.concatenate(
            [
                jnp.concatenate([ends, blank], axis=1),
                jnp.concatenate([blank, ends], axis=1),
            ],
            axis=0,
        )
        tail = nt_dot(beside, weights).reshape(2, 64, 128)
        return jnp.concatenate([main[0], main[1], tail], axis=-1)

    for n, k in enumerate((2, 1, 3)):
        xd = (x + k) % 4
        cx_send[n] = project(xd).astype(BF16)
        remote(
            cx_send.at[n, order[0]], cx_recv.at[0, n], cx_out, cx_sem.at[0], at(x_=xd)
        ).start()
    for n, k in enumerate((2, 1, 3)):
        remote(
            cx_send.at[n, order[1]], cx_recv.at[1, n], cx_out, cx_sem.at[1], at(x_=(x + k) % 4)
        ).start()
    cx_own[...] = project(x)

    lane_half = lax.broadcasted_iota(jnp.int32, (64, 128), 1) // 64
    for i in range(2):
        await_bytes(cx_recv.at[i], cx_sem.at[i])
        total = cx_own[order[i]]
        for n in range(3):
            total = total + cx_recv[i, n].astype(F32)
        ends = total[:, 512:640]
        turned = pltpu.roll(ends, 64, 1)
        for zz in range(2):
            placed = jnp.where(lane_half == yy, jnp.where(yy == zz, ends, turned), 0.0)
            y_send[i, zz, :, :256] = total[:, zz * 256 : zz * 256 + 256].astype(BF16)
            y_send[i, zz, :, 256:] = placed.astype(BF16)
            src, dst = y_send.at[i, zz], y_out_ref.at[yh, yy]
            here = jnp.logical_and(mine, jnp.logical_and(z % 2 == zz, order[i] == yy))

            @pl.when(here)
            def _(src=src, dst=dst):
                pltpu.make_async_copy(src, dst, y_sem).start()

            @pl.when(jnp.logical_not(here))
            def _(src=src, dst=dst, zz=zz, i=i):
                remote(
                    src, dst, y_out, y_sem, at(z_=base + zz, yl_=2 * order[i] + yb, yh_=half)
                ).start()

    await_bytes(y_out_ref, y_sem)

    @pl.when(mine)
    def _():
        await_bytes(b_buf.at[0, pl.ds(0, 192)], y_out)

    @pl.when(jnp.logical_not(mine))
    def _():
        await_bytes(y_out_ref, y_out)

    @pl.when(attends)
    def _():
        await_bytes(emb.at[pl.ds(0, 11)], qkv_out)
        await_bytes(t_send.at[pl.ds(0, 11)], t_out)
        await_bytes(kv_peer, kv_out)
        for i in range(4):

            @pl.when(z // 2 == i)
            def _(i=i):
                await_bytes(kv_peer.at[pl.ds(0, 14)], o_out.at[i])

            @pl.when(z // 2 != i)
            def _(i=i):
                await_bytes(kv_peer.at[pl.ds(0, 16)], o_out.at[i])

    @pl.when(jnp.logical_not(attends))
    def _():
        await_bytes(emb, qkv_out)
        await_bytes(t_send, t_out)

    @pl.when(z % 2 == first)
    def _():
        await_bytes(b_buf.at[pl.ds(0, 3), pl.ds(0, NROWS)], b_out)
        await_bytes(b_buf.at[pl.ds(0, 3), pl.ds(0, YROWS)], bz_out)

    @pl.when(z % 2 != first)
    def _():
        await_bytes(b_buf.at[:, pl.ds(0, NROWS)], b_out)
        await_bytes(b_buf.at[:, pl.ds(0, YROWS)], bz_out)

    await_bytes(near, near_out)
    await_bytes(b_buf.at[:, pl.ds(0, ZROWS)], by_out)
    await_bytes(b_buf.at[:, pl.ds(0, NROWS)], bc_out)
    await_bytes(b_buf.at[:, pl.ds(0, NROWS)], bd_out)
    await_bytes(cx_send, cx_out)


def shards(fresh, still_masked, actions, action_table, mask_vector, position, cache, w_out):
    anywhere = pl.BlockSpec(memory_space=pl.ANY)
    vmem = pl.BlockSpec(memory_space=pltpu.VMEM)
    smem = pl.BlockSpec(memory_space=pltpu.SMEM)
    dma = pltpu.SemaphoreType.DMA
    parts = pl.pallas_call(
        kernel,
        out_shape=jax.ShapeDtypeStruct((2, 2, 64, 384), BF16),
        in_specs=[smem, vmem, vmem, vmem, anywhere, anywhere, anywhere, anywhere],
        out_specs=anywhere,
        scratch_shapes=[
            pltpu.VMEM((3, 4, 16, 384), BF16),
            pltpu.VMEM((3, 16, 384), BF16),
            pltpu.VMEM((2, 16, 4, 16, 384), BF16),
            pltpu.VMEM((NROWS, 384), BF16),
            pltpu.VMEM((12, 3, 16, HD), BF16),
            pltpu.VMEM((32, 3, 16, HD), BF16),
            pltpu.VMEM((32, 2, 16, HD), BF16),
            pltpu.VMEM((12, 16, HD), BF16),
            pltpu.VMEM((32, 16, HD), BF16),
            pltpu.VMEM((4, 2, 2, 2, 16, HD), BF16),
            pltpu.VMEM((3, 2, 2, 4, 16, HD), BF16),
            pltpu.VMEM((YROWS, 384), BF16),
            pltpu.VMEM((4, 4 * NROWS, 384), BF16),
            pltpu.VMEM((3, 2, 64, 640), BF16),
            pltpu.VMEM((2, 64, 640), F32),
            pltpu.VMEM((2, 3, 64, 640), BF16),
            pltpu.VMEM((2, 2, 64, 384), BF16),
            dma((4,)),
            dma((4,)),
            dma((2,)),
        ]
        + [dma] * 22,
        compiler_params=pltpu.CompilerParams(
            collective_id=0, has_side_effects=True, vmem_limit_bytes=60 << 20
        ),
        cost_estimate=pl.CostEstimate(
            flops=400_000_000, bytes_accessed=2_000_000, transcendentals=600_000
        ),
    )(
        actions,
        still_masked,
        jnp.transpose(action_table, (1, 0, 2)),
        mask_vector,
        fresh,
        position,
        cache,
        jnp.transpose(w_out),
    )
    parts = parts[0].astype(F32) + parts[1].astype(F32)
    middle = parts[0, :, 256:] + parts[1, :, 256:]
    return jnp.concatenate([parts[0, :, :256], middle, parts[1, :, :256]], axis=1).reshape(
        4, 16, 640
    )


def solution(mesh):
    placed = (
        P(None, None, "patch", "head"),
        P(None, "patch"),
        P(),
        P(None, None, "head"),
        P(None, "head"),
        P(None, "patch", "head"),
        P(None, None, None, "patch", "head"),
        P("head", "patch"),
    )
    return jax.shard_map(
        shards, mesh=mesh, in_specs=placed, out_specs=P(None, "patch", "head"), check_vma=False
    )
```

```python
import functools

import jax
import jax.numpy as jnp
from jax import lax
from jax.experimental import pallas as pl
from jax.experimental.pallas import tpu as pltpu
from jax.sharding import PartitionSpec as P

HD = 128
NACT = 8
ROLL = 4
FRAMES = 16
SCALE = HD ** (-0.5)
LOG2E = 1.4426950408889634
PLACE = (0, 3, 5)
YPLACE = (0, 1, 2, 3)
ZROWS, YROWS = 32, 48
NROWS = ZROWS + YROWS

BF16, F32 = jnp.bfloat16, jnp.float32


def nt_dot(a, b):
    return lax.dot_general(a, b, (((1,), (1,)), ((), ())), preferred_element_type=F32)


def kernel(
    actions, still_ref, table_ref, maskv_ref, fresh_hbm, pos_hbm, cache_hbm, w_hbm, y_out_ref,
    fresh, pos, cache, w_own, emb, qkv, kv_peer, t_send, t_recv, o_buf, att, near, b_buf,
    cx_send, cx_own, cx_recv, y_send,
    in_sem, o_out, cx_sem, o_sem, qkv_sem, kv_sem, t_sem, near_sem, b_sem, bz_sem, by_sem,
    bc_sem, bd_sem, y_sem,
    qkv_out, kv_out, t_out, near_out, b_out, bz_out, by_out, bc_out, bd_out, cx_out, y_out,
):
    patch, head = lax.axis_index("patch"), lax.axis_index("head")
    z, yl, c = patch // 8, (patch // 2) % 4, patch % 2
    yh, x = head // 4, head % 4
    yy, yb = yl // 2, yl % 2
    half = (z + yy) % 2
    base = (z // 2) * 2

    def at(z_=None, yl_=None, c_=None, yh_=None, x_=None):
        z_, yl_ = z if z_ is None else z_, yl if yl_ is None else yl_
        c_, yh_ = c if c_ is None else c_, yh if yh_ is None else yh_
        x_ = x if x_ is None else x_
        return {"patch": z_ * 8 + yl_ * 2 + c_, "head": yh_ * 4 + x_}

    def remote(src, dst, send, recv, device):
        return pltpu.make_async_remote_copy(
            src_ref=src, dst_ref=dst, send_sem=send, recv_sem=recv,
            device_id=device, device_id_type=pl.DeviceIdType.MESH,
        )

    def await_bytes(ref, sem):
        pltpu.make_async_copy(ref, ref, sem).wait()

    loads = [
        pltpu.make_async_copy(src, dst, in_sem.at[i])
        for i, (src, dst) in enumerate(
            ((fresh_hbm, fresh), (pos_hbm, pos), (w_hbm, w_own), (cache_hbm, cache))
        )
    ]
    for load in loads:
        load.start()

    barrier = pltpu.get_barrier_semaphore()

    def hail(device):
        pl.semaphore_signal(barrier, inc=1, device_id=device, device_id_type=pl.DeviceIdType.MESH)

    def hail_group(i, carry):
        s = (z * 4 + yl + i) % 32
        hail(at(z_=s // 4, yl_=s % 4))
        return carry

    lax.fori_loop(1, 32, hail_group, 0)
    hail(at(c_=1 - c))
    for k in (1, 2, 3):
        hail(at(x_=(x + k) % 4))
    for zz in range(2):
        for w in range(2):
            hail(at(yh_=1 - yh, z_=base + zz, yl_=2 * w + yb))

    loads[0].wait()
    loads[1].wait()
    diagonal = lax.broadcasted_iota(jnp.int32, (16, 16), 0) == lax.broadcasted_iota(
        jnp.int32, (16, 16), 1
    )
    row_of = lax.broadcasted_iota(jnp.int32, (NACT, 384), 0)
    for r in range(ROLL):
        flags = jnp.broadcast_to(still_ref[r : r + 1, :], (16, 16))
        masked = jnp.sum(jnp.where(diagonal, flags, 0).astype(F32), axis=1, keepdims=True) > 0.5
        for i in range(3):
            bias = jnp.sum(
                jnp.where(row_of == actions[r], table_ref[i].astype(F32), 0.0), axis=0, keepdims=True
            )
            mask_row = maskv_ref[i : i + 1, :].astype(F32)
            start = jnp.where(masked, mask_row, fresh[i, r].astype(F32))
            whole = (start + bias + pos[i].astype(F32)).astype(BF16)
            for h in range(3):
                emb[r * 3 + h, i] = whole[:, h * HD : (h + 1) * HD]

    loads[2].wait()
    pl.semaphore_wait(barrier, 39)

    me = z * 4 + yl
    pair_head = jnp.int32(-1)
    pair_roll = jnp.int32(0)
    for r in range(ROLL):
        for h in range(3):
            there = jnp.logical_and((2 * r + PLACE[h]) % 8 == z, yl == YPLACE[r])
            pair_head = jnp.where(there, h, pair_head)
            pair_roll = jnp.where(there, r, pair_roll)
    attends = pair_head >= 0

    def to_attending(src, dst, send, recv, r, h):
        zd = (2 * r + PLACE[h]) % 8
        here = jnp.logical_and(z == zd, yl == YPLACE[r])

        @pl.when(here)
        def _():
            pltpu.make_async_copy(src, dst, recv).start()

        @pl.when(jnp.logical_not(here))
        def _():
            remote(src, dst, send, recv, at(z_=zd, yl_=YPLACE[r])).start()

    for r in (0, 1, 2, 3):
        for h in range(3):
            to_attending(emb.at[r * 3 + h], qkv.at[me], qkv_out, qkv_sem, r, h)

    first = (z // 4 + yy) % 2
    own_rows = pl.multiple_of((yb * 2 + c) * NROWS, 16)
    near_rows = pl.multiple_of(((1 - yb) * 2 + c) * NROWS, 16)

    def spread(src, rows, size, send, recv):
        def one(k, carry):
            zd = first + 2 * k
            dst = b_buf.at[z % 4, pl.ds(rows, size)]

            @pl.when(zd == z)
            def _():
                pltpu.make_async_copy(src, dst, recv).start()

            @pl.when(zd != z)
            def _():
                remote(src, dst, send, recv, at(z_=zd)).start()

            return carry

        lax.fori_loop(0, 4, one, 0)

    remote(
        w_own.at[pl.ds(ZROWS, YROWS)], near, near_out, near_sem, at(yl_=2 * yy + 1 - yb)
    ).start()
    spread(w_own, own_rows, NROWS, b_out, b_sem)

    loads[3].wait()

    def temporal(r, carry):
        for h in range(3):
            lanes = slice(h * HD, (h + 1) * HD)
            q = emb[r * 3 + h, 0].astype(F32)
            own_k = emb[r * 3 + h, 1].astype(F32)
            own_v = emb[r * 3 + h, 2].astype(F32)
            keys = cache[0, :, r, :, lanes].astype(F32)
            s = jnp.sum(q[None] * keys, axis=-1, keepdims=True) * SCALE
            own = jnp.sum(q * own_k, axis=-1, keepdims=True) * SCALE
            peak = jnp.maximum(jnp.max(s, axis=0), own)
            e = jnp.exp(s - peak[None])
            own_e = jnp.exp(own - peak)
            total = jnp.sum(e, axis=0) + own_e
            weights = e.astype(BF16).astype(F32)
            values = cache[1, :, r, :, lanes].astype(F32)
            summed = jnp.sum(weights * values, axis=0)
            summed = summed + own_e.astype(BF16).astype(F32) * own_v
            t_send[r * 3 + h] = (summed / total).astype(BF16)
        return carry

    lax.fori_loop(0, ROLL, temporal, 0)

    for r in range(ROLL):
        for h in range(3):
            to_attending(t_send.at[r * 3 + h], t_recv.at[me], t_out, t_sem, r, h)

    await_bytes(near, near_sem)
    spread(near, near_rows + ZROWS, YROWS, bz_out, bz_sem)

    @pl.when(attends)
    def _():
        await_bytes(qkv, qkv_sem)
        remote(qkv.at[:, pl.ds(1, 2)], kv_peer, kv_out, kv_sem, at(c_=1 - c)).start()

    await_bytes(b_buf.at[:, pl.ds(own_rows, NROWS)], b_sem)
    went = b_buf.at[:, pl.ds(own_rows, ZROWS)]
    remote(went, went, by_out, by_sem, at(yl_=2 * yy + 1 - yb)).start()
    gathered = b_buf.at[:, pl.ds(own_rows, NROWS)]
    remote(gathered, gathered, bc_out, bc_sem, at(c_=1 - c)).start()

    @pl.when(attends)
    def _():
        await_bytes(kv_peer, kv_sem)
        await_bytes(t_recv, t_sem)
        c2 = SCALE * LOG2E

        def attend(i, carry):
            q = qkv[pl.ds(i * 8, 8), 0].reshape(128, HD)
            s_a = nt_dot(q, qkv[:, 1].reshape(512, HD))
            s_b = nt_dot(q, kv_peer[:, 0].reshape(512, HD))
            peak = jnp.maximum(
                jnp.max(s_a, axis=-1, keepdims=True), jnp.max(s_b, axis=-1, keepdims=True)
            )
            e_a = jnp.exp2((s_a - peak) * c2)
            e_b = jnp.exp2((s_b - peak) * c2)
            total = jnp.sum(e_a, axis=-1, keepdims=True) + jnp.sum(e_b, axis=-1, keepdims=True)
            o = jnp.dot(
                e_a.astype(BF16), qkv[:, 2].reshape(512, HD), preferred_element_type=F32
            ) + jnp.dot(
                e_b.astype(BF16), kv_peer[:, 1].reshape(512, HD), preferred_element_type=F32
            )
            o = o / total + t_recv[pl.ds(i * 8, 8)].astype(F32).reshape(128, HD)
            o_buf[i] = o.astype(BF16).reshape(2, 2, 2, 16, HD)
            for b in range(2):
                for yd in range(4):
                    zd = 2 * i + b
                    here = jnp.logical_and(zd == z, yl == yd)
                    src, dst = o_buf.at[i, :, :, yd % 2], att.at[pair_head, :, :, pair_roll]

                    @pl.when(here)
                    def _(src=src, dst=dst):
                        pltpu.make_async_copy(src, dst, o_sem.at[pair_roll // 2]).start()

                    @pl.when(jnp.logical_not(here))
                    def _(src=src, dst=dst, zd=zd, yd=yd):
                        remote(
                            src, dst, o_out.at[i], o_sem.at[pair_roll // 2], at(z_=zd, yl_=yd)
                        ).start()

            return carry

        lax.fori_loop(0, 4, attend, 0)

    await_bytes(b_buf.at[:, pl.ds(near_rows, ZROWS)], by_sem)
    await_bytes(b_buf.at[:, pl.ds(near_rows, YROWS)], bz_sem)
    gathered_near = b_buf.at[:, pl.ds(near_rows, NROWS)]
    remote(gathered_near, gathered_near, bd_out, bd_sem, at(c_=1 - c)).start()

    await_bytes(b_buf.at[:, pl.ds(own_rows, NROWS)], bc_sem)
    await_bytes(b_buf.at[:, pl.ds(near_rows, NROWS)], bd_sem)
    blank = jnp.zeros((64, 384), BF16)
    main_rows = pl.multiple_of(yy * 64, 64)
    tail_rows = pl.multiple_of((1 - yy) * 256, 64)
    mine = yh == half
    early = jnp.where(mine, 1 - yy, yy)
    order = (early, 1 - early)
    spans = [pl.ds(pl.multiple_of(order[i] * 32, 32), 32) for i in range(2)]

    for w in range(2):
        await_bytes(att.at[:, :, :, pl.ds(2 * w, 2)], o_sem.at[w])
        tokens = [
            jnp.concatenate(
                [att[h, zz, :, 2 * w : 2 * w + 2].reshape(64, HD) for h in range(3)], axis=1
            )
            for zz in range(2)
        ]
        stacked = jnp.concatenate(tokens, axis=0)
        beside = jnp.concatenate(tokens, axis=1)

        def project(xd, stacked=stacked, beside=beside):
            main = nt_dot(stacked, b_buf[xd, pl.ds(main_rows, 256), :])
            ends = b_buf[xd, pl.ds(tail_rows, 64), :]
            weights = jnp.concatenate(
                [
                    jnp.concatenate([ends, blank], axis=1),
                    jnp.concatenate([blank, ends], axis=1),
                ],
                axis=0,
            )
            return jnp.concatenate([main[:64], main[64:], nt_dot(beside, weights)], axis=1)

        def to_x(i, n, k, w=w):
            remote(
                cx_send.at[w, n, spans[i]], cx_recv.at[w, i, n], cx_out, cx_sem.at[2 * w + i],
                at(x_=(x + k) % 4),
            ).start()

        for n, k in enumerate((2, 1, 3)):
            cx_send[w, n] = project((x + k) % 4).astype(BF16)
            to_x(0, n, k)
        for n, k in enumerate((2, 1, 3)):
            to_x(1, n, k)
        cx_own[w] = project(x)

    lane_half = lax.broadcasted_iota(jnp.int32, (32, 128), 1) // 64
    main_lanes = pl.multiple_of(yy * 128, 128)
    tail_lanes = pl.multiple_of((1 - yy) * 256, 128)
    for w in range(2):
        for i in range(2):
            await_bytes(cx_recv.at[w, i], cx_sem.at[2 * w + i])
            total = cx_own[w, spans[i]]
            for n in range(3):
                total = total + cx_recv[w, i, n].astype(F32)
            ends = total[:, 512:640]
            turned = pltpu.roll(ends, 64, 1)
            for zz in range(2):
                placed = jnp.where(lane_half == yy, jnp.where(yy == zz, ends, turned), 0.0)
                y_send[w, i, zz, :, pl.ds(main_lanes, 256)] = total[
                    :, zz * 256 : zz * 256 + 256
                ].astype(BF16)
                y_send[w, i, zz, :, pl.ds(tail_lanes, 128)] = placed.astype(BF16)
                src, dst = y_send.at[w, i, zz], y_out_ref.at[yh, yy, w]
                here = jnp.logical_and(mine, jnp.logical_and(z % 2 == zz, order[i] == yy))

                @pl.when(here)
                def _(src=src, dst=dst):
                    pltpu.make_async_copy(src, dst, y_sem).start()

                @pl.when(jnp.logical_not(here))
                def _(src=src, dst=dst, zz=zz, i=i):
                    remote(
                        src, dst, y_out, y_sem, at(z_=base + zz, yl_=2 * order[i] + yb, yh_=half)
                    ).start()

    await_bytes(y_out_ref, y_sem)

    @pl.when(mine)
    def _():
        await_bytes(b_buf.at[0, pl.ds(0, 192)], y_out)

    @pl.when(jnp.logical_not(mine))
    def _():
        await_bytes(y_out_ref, y_out)

    @pl.when(attends)
    def _():
        await_bytes(emb.at[pl.ds(0, 11)], qkv_out)
        await_bytes(t_send.at[pl.ds(0, 11)], t_out)
        await_bytes(kv_peer, kv_out)
        for i in range(4):

            @pl.when(z // 2 == i)
            def _(i=i):
                await_bytes(kv_peer.at[pl.ds(0, 14)], o_out.at[i])

            @pl.when(z // 2 != i)
            def _(i=i):
                await_bytes(kv_peer.at[pl.ds(0, 16)], o_out.at[i])

    @pl.when(jnp.logical_not(attends))
    def _():
        await_bytes(emb, qkv_out)
        await_bytes(t_send, t_out)

    @pl.when(z % 2 == first)
    def _():
        await_bytes(b_buf.at[pl.ds(0, 3), pl.ds(0, NROWS)], b_out)
        await_bytes(b_buf.at[pl.ds(0, 3), pl.ds(0, YROWS)], bz_out)

    @pl.when(z % 2 != first)
    def _():
        await_bytes(b_buf.at[:, pl.ds(0, NROWS)], b_out)
        await_bytes(b_buf.at[:, pl.ds(0, YROWS)], bz_out)

    await_bytes(near, near_out)
    await_bytes(b_buf.at[:, pl.ds(0, ZROWS)], by_out)
    await_bytes(b_buf.at[:, pl.ds(0, NROWS)], bc_out)
    await_bytes(b_buf.at[:, pl.ds(0, NROWS)], bd_out)
    await_bytes(cx_send, cx_out)


def shards(fresh, still_masked, actions, action_table, mask_vector, position, cache, w_out):
    anywhere = pl.BlockSpec(memory_space=pl.ANY)
    vmem = pl.BlockSpec(memory_space=pltpu.VMEM)
    smem = pl.BlockSpec(memory_space=pltpu.SMEM)
    dma = pltpu.SemaphoreType.DMA
    parts = pl.pallas_call(
        kernel,
        out_shape=jax.ShapeDtypeStruct((2, 2, 2, 32, 384), BF16),
        in_specs=[smem, vmem, vmem, vmem, anywhere, anywhere, anywhere, anywhere],
        out_specs=anywhere,
        scratch_shapes=[
            pltpu.VMEM((3, 4, 16, 384), BF16),
            pltpu.VMEM((3, 16, 384), BF16),
            pltpu.VMEM((2, 16, 4, 16, 384), BF16),
            pltpu.VMEM((NROWS, 384), BF16),
            pltpu.VMEM((12, 3, 16, HD), BF16),
            pltpu.VMEM((32, 3, 16, HD), BF16),
            pltpu.VMEM((32, 2, 16, HD), BF16),
            pltpu.VMEM((12, 16, HD), BF16),
            pltpu.VMEM((32, 16, HD), BF16),
            pltpu.VMEM((4, 2, 2, 2, 16, HD), BF16),
            pltpu.VMEM((3, 2, 2, 4, 16, HD), BF16),
            pltpu.VMEM((YROWS, 384), BF16),
            pltpu.VMEM((4, 4 * NROWS, 384), BF16),
            pltpu.VMEM((2, 3, 64, 640), BF16),
            pltpu.VMEM((2, 64, 640), F32),
            pltpu.VMEM((2, 2, 3, 32, 640), BF16),
            pltpu.VMEM((2, 2, 2, 32, 384), BF16),
            dma((4,)),
            dma((4,)),
            dma((4,)),
            dma((2,)),
        ]
        + [dma] * 21,
        compiler_params=pltpu.CompilerParams(
            collective_id=0, has_side_effects=True, vmem_limit_bytes=60 << 20
        ),
        cost_estimate=pl.CostEstimate(
            flops=400_000_000, bytes_accessed=2_000_000, transcendentals=600_000
        ),
    )(
        actions,
        still_masked,
        jnp.transpose(action_table, (1, 0, 2)),
        mask_vector,
        fresh,
        position,
        cache,
        jnp.transpose(w_out),
    )
    parts = parts.reshape(2, 2, 64, 384)
    return sum(
        jnp.pad(parts[k, b].astype(F32), ((0, 0), (256 * b, 256 * (1 - b))))
        for k in range(2)
        for b in range(2)
    ).reshape(4, 16, 640)


def solution(mesh):
    placed = (
        P(None, None, "patch", "head"),
        P(None, "patch"),
        P(),
        P(None, None, "head"),
        P(None, "head"),
        P(None, "patch", "head"),
        P(None, None, None, "patch", "head"),
        P("head", "patch"),
    )
    return jax.shard_map(
        shards, mesh=mesh, in_specs=placed, out_specs=P(None, "patch", "head"), check_vma=False
    )
```

```python
import functools

import jax
import jax.numpy as jnp
from jax import lax
from jax.experimental import pallas as pl
from jax.experimental.pallas import tpu as pltpu
from jax.sharding import PartitionSpec as P

HD = 128
NACT = 8
ROLL = 4
FRAMES = 16
SCALE = HD ** (-0.5)
LOG2E = 1.4426950408889634
PLACE = (0, 3, 5)
YPLACE = (0, 1, 2, 3)
ZROWS, YROWS = 32, 48
NROWS = ZROWS + YROWS

BF16, F32 = jnp.bfloat16, jnp.float32


def nt_dot(a, b):
    return lax.dot_general(a, b, (((1,), (1,)), ((), ())), preferred_element_type=F32)


def kernel(
    actions, still_ref, table_ref, maskv_ref, fresh_hbm, pos_hbm, cache_hbm, w_hbm, y_out_ref,
    fresh, pos, cache, w_own, emb, qkv, kv_peer, t_send, t_recv, o_buf, att, near, b_buf,
    cx_send, cx_own, cx_recv, y_send,
    in_sem, o_out, cx_sem, o_sem, qkv_sem, kv_sem, t_sem, near_sem, b_sem, bz_sem, by_sem,
    bc_sem, bd_sem, y_sem,
    qkv_out, kv_out, t_out, near_out, b_out, bz_out, by_out, bc_out, bd_out, cx_out, y_out,
):
    patch, head = lax.axis_index("patch"), lax.axis_index("head")
    z, yl, c = patch // 8, (patch // 2) % 4, patch % 2
    yh, x = head // 4, head % 4
    yy, yb = yl // 2, yl % 2
    half = (z + yy) % 2
    base = (z // 2) * 2

    def at(z_=None, yl_=None, c_=None, yh_=None, x_=None):
        z_, yl_ = z if z_ is None else z_, yl if yl_ is None else yl_
        c_, yh_ = c if c_ is None else c_, yh if yh_ is None else yh_
        x_ = x if x_ is None else x_
        return {"patch": z_ * 8 + yl_ * 2 + c_, "head": yh_ * 4 + x_}

    def remote(src, dst, send, recv, device):
        return pltpu.make_async_remote_copy(
            src_ref=src, dst_ref=dst, send_sem=send, recv_sem=recv,
            device_id=device, device_id_type=pl.DeviceIdType.MESH,
        )

    def await_bytes(ref, sem):
        pltpu.make_async_copy(ref, ref, sem).wait()

    loads = [
        pltpu.make_async_copy(src, dst, in_sem.at[i])
        for i, (src, dst) in enumerate(
            ((fresh_hbm, fresh), (pos_hbm, pos), (w_hbm, w_own), (cache_hbm, cache))
        )
    ]
    for load in loads:
        load.start()

    barrier = pltpu.get_barrier_semaphore()

    def hail(device):
        pl.semaphore_signal(barrier, inc=1, device_id=device, device_id_type=pl.DeviceIdType.MESH)

    def hail_group(i, carry):
        s = (z * 4 + yl + i) % 32
        hail(at(z_=s // 4, yl_=s % 4))
        return carry

    for i in (16, 15, 17, 14, 18, 13, 19, 12, 20, 11, 21, 10, 22, 9, 23, 8, 24, 7, 25, 6, 26, 5, 27, 4, 28, 3, 29, 2, 30, 1, 31):
        hail_group(i, 0)
    hail(at(c_=1 - c))
    for k in (1, 2, 3):
        hail(at(x_=(x + k) % 4))
    for zz in range(2):
        for w in range(2):
            hail(at(yh_=1 - yh, z_=base + zz, yl_=2 * w + yb))

    loads[0].wait()
    loads[1].wait()
    diagonal = lax.broadcasted_iota(jnp.int32, (16, 16), 0) == lax.broadcasted_iota(
        jnp.int32, (16, 16), 1
    )
    row_of = lax.broadcasted_iota(jnp.int32, (NACT, 384), 0)
    for r in range(ROLL):
        flags = jnp.broadcast_to(still_ref[r : r + 1, :], (16, 16))
        masked = jnp.sum(jnp.where(diagonal, flags, 0).astype(F32), axis=1, keepdims=True) > 0.5
        for i in range(3):
            bias = jnp.sum(
                jnp.where(row_of == actions[r], table_ref[i].astype(F32), 0.0), axis=0, keepdims=True
            )
            mask_row = maskv_ref[i : i + 1, :].astype(F32)
            start = jnp.where(masked, mask_row, fresh[i, r].astype(F32))
            whole = (start + bias + pos[i].astype(F32)).astype(BF16)
            for h in range(3):
                emb[r * 3 + h, i] = whole[:, h * HD : (h + 1) * HD]

    loads[2].wait()
    pl.semaphore_wait(barrier, 39)

    me = z * 4 + yl
    pair_head = jnp.int32(-1)
    pair_roll = jnp.int32(0)
    for r in range(ROLL):
        for h in range(3):
            there = jnp.logical_and((2 * r + PLACE[h]) % 8 == z, yl == YPLACE[r])
            pair_head = jnp.where(there, h, pair_head)
            pair_roll = jnp.where(there, r, pair_roll)
    attends = pair_head >= 0

    def to_attending(src, dst, send, recv, r, h):
        zd = (2 * r + PLACE[h]) % 8
        here = jnp.logical_and(z == zd, yl == YPLACE[r])

        @pl.when(here)
        def _():
            pltpu.make_async_copy(src, dst, recv).start()

        @pl.when(jnp.logical_not(here))
        def _():
            remote(src, dst, send, recv, at(z_=zd, yl_=YPLACE[r])).start()

    for r in (0, 1, 2, 3):
        for h in range(3):
            to_attending(emb.at[r * 3 + h], qkv.at[me], qkv_out, qkv_sem, r, h)

    first = (z // 4 + yy) % 2
    own_rows = pl.multiple_of((yb * 2 + c) * NROWS, 16)
    near_rows = pl.multiple_of(((1 - yb) * 2 + c) * NROWS, 16)

    def spread(src, rows, size, send, recv):
        def one(k, carry):
            zd = first + 2 * k
            dst = b_buf.at[z % 4, pl.ds(rows, size)]

            @pl.when(zd == z)
            def _():
                pltpu.make_async_copy(src, dst, recv).start()

            @pl.when(zd != z)
            def _():
                remote(src, dst, send, recv, at(z_=zd)).start()

            return carry

        lax.fori_loop(0, 4, one, 0)

    remote(
        w_own.at[pl.ds(ZROWS, YROWS)], near, near_out, near_sem, at(yl_=2 * yy + 1 - yb)
    ).start()
    spread(w_own, own_rows, NROWS, b_out, b_sem)

    loads[3].wait()

    def temporal(r, carry):
        for h in range(3):
            lanes = slice(h * HD, (h + 1) * HD)
            q = emb[r * 3 + h, 0].astype(F32)
            own_k = emb[r * 3 + h, 1].astype(F32)
            own_v = emb[r * 3 + h, 2].astype(F32)
            keys = cache[0, :, r, :, lanes].astype(F32)
            s = jnp.sum(q[None] * keys, axis=-1, keepdims=True) * SCALE
            own = jnp.sum(q * own_k, axis=-1, keepdims=True) * SCALE
            peak = jnp.maximum(jnp.max(s, axis=0), own)
            e = jnp.exp(s - peak[None])
            own_e = jnp.exp(own - peak)
            total = jnp.sum(e, axis=0) + own_e
            weights = e.astype(BF16).astype(F32)
            values = cache[1, :, r, :, lanes].astype(F32)
            summed = jnp.sum(weights * values, axis=0)
            summed = summed + own_e.astype(BF16).astype(F32) * own_v
            t_send[r * 3 + h] = (summed / total).astype(BF16)
        return carry

    lax.fori_loop(0, ROLL, temporal, 0)

    for r in range(ROLL):
        for h in range(3):
            to_attending(t_send.at[r * 3 + h], t_recv.at[me], t_out, t_sem, r, h)

    await_bytes(near, near_sem)
    spread(near, near_rows + ZROWS, YROWS, bz_out, bz_sem)

    @pl.when(attends)
    def _():
        await_bytes(qkv, qkv_sem)
        remote(qkv.at[:, pl.ds(1, 2)], kv_peer, kv_out, kv_sem, at(c_=1 - c)).start()

    await_bytes(b_buf.at[:, pl.ds(own_rows, NROWS)], b_sem)
    went = b_buf.at[:, pl.ds(own_rows, ZROWS)]
    remote(went, went, by_out, by_sem, at(yl_=2 * yy + 1 - yb)).start()
    gathered = b_buf.at[:, pl.ds(own_rows, NROWS)]
    remote(gathered, gathered, bc_out, bc_sem, at(c_=1 - c)).start()

    @pl.when(attends)
    def _():
        await_bytes(kv_peer, kv_sem)
        await_bytes(t_recv, t_sem)
        c2 = SCALE * LOG2E

        def attend(i, carry):
            q = qkv[pl.ds(i * 8, 8), 0].reshape(128, HD)
            s_a = nt_dot(q, qkv[:, 1].reshape(512, HD))
            s_b = nt_dot(q, kv_peer[:, 0].reshape(512, HD))
            peak = jnp.maximum(
                jnp.max(s_a, axis=-1, keepdims=True), jnp.max(s_b, axis=-1, keepdims=True)
            )
            e_a = jnp.exp2((s_a - peak) * c2)
            e_b = jnp.exp2((s_b - peak) * c2)
            total = jnp.sum(e_a, axis=-1, keepdims=True) + jnp.sum(e_b, axis=-1, keepdims=True)
            o = jnp.dot(
                e_a.astype(BF16), qkv[:, 2].reshape(512, HD), preferred_element_type=F32
            ) + jnp.dot(
                e_b.astype(BF16), kv_peer[:, 1].reshape(512, HD), preferred_element_type=F32
            )
            o = o / total + t_recv[pl.ds(i * 8, 8)].astype(F32).reshape(128, HD)
            o_buf[i] = o.astype(BF16).reshape(2, 2, 2, 16, HD)
            for b in range(2):
                for step in (2, 1, 3, 0):
                    yd = (yl + step) % 4
                    zd = 2 * i + b
                    here = jnp.logical_and(zd == z, yl == yd)
                    src, dst = o_buf.at[i, :, :, (yl + step) % 2], att.at[pair_head, :, :, pair_roll]

                    @pl.when(here)
                    def _(src=src, dst=dst):
                        pltpu.make_async_copy(src, dst, o_sem.at[pair_roll // 2]).start()

                    @pl.when(jnp.logical_not(here))
                    def _(src=src, dst=dst, zd=zd, yd=yd):
                        remote(
                            src, dst, o_out.at[i], o_sem.at[pair_roll // 2], at(z_=zd, yl_=yd)
                        ).start()

            return carry

        lax.fori_loop(0, 4, attend, 0)

    await_bytes(b_buf.at[:, pl.ds(near_rows, ZROWS)], by_sem)
    await_bytes(b_buf.at[:, pl.ds(near_rows, YROWS)], bz_sem)
    gathered_near = b_buf.at[:, pl.ds(near_rows, NROWS)]
    remote(gathered_near, gathered_near, bd_out, bd_sem, at(c_=1 - c)).start()

    await_bytes(b_buf.at[:, pl.ds(own_rows, NROWS)], bc_sem)
    await_bytes(b_buf.at[:, pl.ds(near_rows, NROWS)], bd_sem)
    blank = jnp.zeros((64, 384), BF16)
    main_rows = pl.multiple_of(yy * 64, 64)
    tail_rows = pl.multiple_of((1 - yy) * 256, 64)
    mine = yh == half
    early = jnp.where(mine, 1 - yy, yy)
    order = (early, 1 - early)
    spans = [pl.ds(pl.multiple_of(order[i] * 32, 32), 32) for i in range(2)]

    for w in range(2):
        await_bytes(att.at[:, :, :, pl.ds(2 * w, 2)], o_sem.at[w])
        tokens = [
            jnp.concatenate(
                [att[h, zz, :, 2 * w : 2 * w + 2].reshape(64, HD) for h in range(3)], axis=1
            )
            for zz in range(2)
        ]
        stacked = jnp.concatenate(tokens, axis=0)
        beside = jnp.concatenate(tokens, axis=1)

        def project(xd, stacked=stacked, beside=beside):
            main = nt_dot(stacked, b_buf[xd, pl.ds(main_rows, 256), :])
            ends = b_buf[xd, pl.ds(tail_rows, 64), :]
            weights = jnp.concatenate(
                [
                    jnp.concatenate([ends, blank], axis=1),
                    jnp.concatenate([blank, ends], axis=1),
                ],
                axis=0,
            )
            return jnp.concatenate([main[:64], main[64:], nt_dot(beside, weights)], axis=1)

        def to_x(i, n, k, w=w):
            remote(
                cx_send.at[w, n, spans[i]], cx_recv.at[w, i, n], cx_out, cx_sem.at[2 * w + i],
                at(x_=(x + k) % 4),
            ).start()

        for n, k in enumerate((2, 3, 1)):
            cx_send[w, n] = project((x + k) % 4).astype(BF16)
            to_x(0, n, k)
        for n, k in enumerate((2, 3, 1)):
            to_x(1, n, k)
        cx_own[w] = project(x)

    lane_half = lax.broadcasted_iota(jnp.int32, (32, 128), 1) // 64
    main_lanes = pl.multiple_of(yy * 128, 128)
    tail_lanes = pl.multiple_of((1 - yy) * 256, 128)
    for w in range(2):
        for i in range(2):
            await_bytes(cx_recv.at[w, i], cx_sem.at[2 * w + i])
            total = cx_own[w, spans[i]]
            for n in range(3):
                total = total + cx_recv[w, i, n].astype(F32)
            ends = total[:, 512:640]
            turned = pltpu.roll(ends, 64, 1)
            for zz in range(2):
                placed = jnp.where(lane_half == yy, jnp.where(yy == zz, ends, turned), 0.0)
                y_send[w, i, zz, :, pl.ds(main_lanes, 256)] = total[
                    :, zz * 256 : zz * 256 + 256
                ].astype(BF16)
                y_send[w, i, zz, :, pl.ds(tail_lanes, 128)] = placed.astype(BF16)
                src, dst = y_send.at[w, i, zz], y_out_ref.at[yh, yy, w]
                here = jnp.logical_and(mine, jnp.logical_and(z % 2 == zz, order[i] == yy))

                @pl.when(here)
                def _(src=src, dst=dst):
                    pltpu.make_async_copy(src, dst, y_sem).start()

                @pl.when(jnp.logical_not(here))
                def _(src=src, dst=dst, zz=zz, i=i):
                    remote(
                        src, dst, y_out, y_sem, at(z_=base + zz, yl_=2 * order[i] + yb, yh_=half)
                    ).start()

    await_bytes(y_out_ref, y_sem)

    @pl.when(mine)
    def _():
        await_bytes(b_buf.at[0, pl.ds(0, 192)], y_out)

    @pl.when(jnp.logical_not(mine))
    def _():
        await_bytes(y_out_ref, y_out)

    @pl.when(attends)
    def _():
        await_bytes(emb.at[pl.ds(0, 11)], qkv_out)
        await_bytes(t_send.at[pl.ds(0, 11)], t_out)
        await_bytes(kv_peer, kv_out)
        for i in range(4):

            @pl.when(z // 2 == i)
            def _(i=i):
                await_bytes(kv_peer.at[pl.ds(0, 14)], o_out.at[i])

            @pl.when(z // 2 != i)
            def _(i=i):
                await_bytes(kv_peer.at[pl.ds(0, 16)], o_out.at[i])

    @pl.when(jnp.logical_not(attends))
    def _():
        await_bytes(emb, qkv_out)
        await_bytes(t_send, t_out)

    @pl.when(z % 2 == first)
    def _():
        await_bytes(b_buf.at[pl.ds(0, 3), pl.ds(0, NROWS)], b_out)
        await_bytes(b_buf.at[pl.ds(0, 3), pl.ds(0, YROWS)], bz_out)

    @pl.when(z % 2 != first)
    def _():
        await_bytes(b_buf.at[:, pl.ds(0, NROWS)], b_out)
        await_bytes(b_buf.at[:, pl.ds(0, YROWS)], bz_out)

    await_bytes(near, near_out)
    await_bytes(b_buf.at[:, pl.ds(0, ZROWS)], by_out)
    await_bytes(b_buf.at[:, pl.ds(0, NROWS)], bc_out)
    await_bytes(b_buf.at[:, pl.ds(0, NROWS)], bd_out)
    await_bytes(cx_send, cx_out)


def shards(fresh, still_masked, actions, action_table, mask_vector, position, cache, w_out):
    anywhere = pl.BlockSpec(memory_space=pl.ANY)
    vmem = pl.BlockSpec(memory_space=pltpu.VMEM)
    smem = pl.BlockSpec(memory_space=pltpu.SMEM)
    dma = pltpu.SemaphoreType.DMA
    parts = pl.pallas_call(
        kernel,
        out_shape=jax.ShapeDtypeStruct((2, 2, 2, 32, 384), BF16),
        in_specs=[smem, vmem, vmem, vmem, anywhere, anywhere, anywhere, anywhere],
        out_specs=anywhere,
        scratch_shapes=[
            pltpu.VMEM((3, 4, 16, 384), BF16),
            pltpu.VMEM((3, 16, 384), BF16),
            pltpu.VMEM((2, 16, 4, 16, 384), BF16),
            pltpu.VMEM((NROWS, 384), BF16),
            pltpu.VMEM((12, 3, 16, HD), BF16),
            pltpu.VMEM((32, 3, 16, HD), BF16),
            pltpu.VMEM((32, 2, 16, HD), BF16),
            pltpu.VMEM((12, 16, HD), BF16),
            pltpu.VMEM((32, 16, HD), BF16),
            pltpu.VMEM((4, 2, 2, 2, 16, HD), BF16),
            pltpu.VMEM((3, 2, 2, 4, 16, HD), BF16),
            pltpu.VMEM((YROWS, 384), BF16),
            pltpu.VMEM((4, 4 * NROWS, 384), BF16),
            pltpu.VMEM((2, 3, 64, 640), BF16),
            pltpu.VMEM((2, 64, 640), F32),
            pltpu.VMEM((2, 2, 3, 32, 640), BF16),
            pltpu.VMEM((2, 2, 2, 32, 384), BF16),
            dma((4,)),
            dma((4,)),
            dma((4,)),
            dma((2,)),
        ]
        + [dma] * 21,
        compiler_params=pltpu.CompilerParams(
            collective_id=0, has_side_effects=True, vmem_limit_bytes=60 << 20
        ),
        cost_estimate=pl.CostEstimate(
            flops=400_000_000, bytes_accessed=2_000_000, transcendentals=600_000
        ),
    )(
        actions,
        still_masked,
        jnp.transpose(action_table, (1, 0, 2)),
        mask_vector,
        fresh,
        position,
        cache,
        jnp.transpose(w_out),
    )
    parts = parts.reshape(2, 2, 64, 384)
    return sum(
        jnp.pad(parts[k, b].astype(F32), ((0, 0), (256 * b, 256 * (1 - b))))
        for k in range(2)
        for b in range(2)
    ).reshape(4, 16, 640)


def solution(mesh):
    placed = (
        P(None, None, "patch", "head"),
        P(None, "patch"),
        P(),
        P(None, None, "head"),
        P(None, "head"),
        P(None, "patch", "head"),
        P(None, None, None, "patch", "head"),
        P("head", "patch"),
    )
    return jax.shard_map(
        shards, mesh=mesh, in_specs=placed, out_specs=P(None, "patch", "head"), check_vma=False
    )
```

```python
import functools

import jax
import jax.numpy as jnp
from jax import lax
from jax.experimental import pallas as pl
from jax.experimental.pallas import tpu as pltpu
from jax.sharding import PartitionSpec as P

HD = 128
NACT = 8
ROLL = 4
FRAMES = 16
SCALE = HD ** (-0.5)
LOG2E = 1.4426950408889634
PLACE = ((0, 3, 5), (2, 5, 7), (1, 4, 6), (0, 3, 6))
YPLACE = (0, 1, 2, 3)
ZROWS, YROWS = 32, 48
NROWS = ZROWS + YROWS

BF16, F32 = jnp.bfloat16, jnp.float32


def nt_dot(a, b):
    return lax.dot_general(a, b, (((1,), (1,)), ((), ())), preferred_element_type=F32)


def kernel(
    actions, still_ref, table_ref, maskv_ref, fresh_hbm, pos_hbm, cache_hbm, w_hbm, y_out_ref,
    fresh, pos, cache, w_own, emb, qkv, kv_peer, t_send, t_recv, o_buf, att, near, b_buf,
    cx_send, cx_own, cx_recv, y_send,
    in_sem, o_out, cx_sem, o_sem, qkv_sem, kv_sem, t_sem, near_sem, b_sem, bz_sem, by_sem,
    bc_sem, bd_sem, y_sem,
    qkv_out, kv_out, t_out, near_out, b_out, bz_out, by_out, bc_out, bd_out, cx_out, y_out,
):
    patch, head = lax.axis_index("patch"), lax.axis_index("head")
    z, yl, c = patch // 8, (patch // 2) % 4, patch % 2
    yh, x = head // 4, head % 4
    yy, yb = yl // 2, yl % 2
    half = (z + yy) % 2
    base = (z // 2) * 2

    def at(z_=None, yl_=None, c_=None, yh_=None, x_=None):
        z_, yl_ = z if z_ is None else z_, yl if yl_ is None else yl_
        c_, yh_ = c if c_ is None else c_, yh if yh_ is None else yh_
        x_ = x if x_ is None else x_
        return {"patch": z_ * 8 + yl_ * 2 + c_, "head": yh_ * 4 + x_}

    def remote(src, dst, send, recv, device):
        return pltpu.make_async_remote_copy(
            src_ref=src, dst_ref=dst, send_sem=send, recv_sem=recv,
            device_id=device, device_id_type=pl.DeviceIdType.MESH,
        )

    def await_bytes(ref, sem):
        pltpu.make_async_copy(ref, ref, sem).wait()

    loads = [
        pltpu.make_async_copy(src, dst, in_sem.at[i])
        for i, (src, dst) in enumerate(
            ((fresh_hbm, fresh), (pos_hbm, pos), (w_hbm, w_own), (cache_hbm, cache))
        )
    ]
    for load in loads:
        load.start()

    barrier = pltpu.get_barrier_semaphore()

    def hail(device):
        pl.semaphore_signal(barrier, inc=1, device_id=device, device_id_type=pl.DeviceIdType.MESH)

    def hail_group(i, carry):
        s = (z * 4 + yl + i) % 32
        hail(at(z_=s // 4, yl_=s % 4))
        return carry

    for i in (16, 15, 17, 14, 18, 13, 19, 12, 20, 11, 21, 10, 22, 9, 23, 8, 24, 7, 25, 6, 26, 5, 27, 4, 28, 3, 29, 2, 30, 1, 31):
        hail_group(i, 0)
    hail(at(c_=1 - c))
    for k in (1, 2, 3):
        hail(at(x_=(x + k) % 4))
    for zz in range(2):
        for w in range(2):
            hail(at(yh_=1 - yh, z_=base + zz, yl_=2 * w + yb))

    loads[0].wait()
    loads[1].wait()
    diagonal = lax.broadcasted_iota(jnp.int32, (16, 16), 0) == lax.broadcasted_iota(
        jnp.int32, (16, 16), 1
    )
    row_of = lax.broadcasted_iota(jnp.int32, (NACT, 384), 0)
    for r in range(ROLL):
        flags = jnp.broadcast_to(still_ref[r : r + 1, :], (16, 16))
        masked = jnp.sum(jnp.where(diagonal, flags, 0).astype(F32), axis=1, keepdims=True) > 0.5
        for i in range(3):
            bias = jnp.sum(
                jnp.where(row_of == actions[r], table_ref[i].astype(F32), 0.0), axis=0, keepdims=True
            )
            mask_row = maskv_ref[i : i + 1, :].astype(F32)
            start = jnp.where(masked, mask_row, fresh[i, r].astype(F32))
            whole = (start + bias + pos[i].astype(F32)).astype(BF16)
            for h in range(3):
                emb[r * 3 + h, i] = whole[:, h * HD : (h + 1) * HD]

    loads[2].wait()
    pl.semaphore_wait(barrier, 39)

    me = z * 4 + yl
    pair_head = jnp.int32(-1)
    pair_roll = jnp.int32(0)
    for r in range(ROLL):
        for h in range(3):
            there = jnp.logical_and(PLACE[r][h] == z, yl == YPLACE[r])
            pair_head = jnp.where(there, h, pair_head)
            pair_roll = jnp.where(there, r, pair_roll)
    attends = pair_head >= 0

    def to_attending(src, dst, send, recv, r, h):
        zd = PLACE[r][h]
        here = jnp.logical_and(z == zd, yl == YPLACE[r])

        @pl.when(here)
        def _():
            pltpu.make_async_copy(src, dst, recv).start()

        @pl.when(jnp.logical_not(here))
        def _():
            remote(src, dst, send, recv, at(z_=zd, yl_=YPLACE[r])).start()

    for r in (0, 1, 2, 3):
        for h in range(3):
            to_attending(emb.at[r * 3 + h], qkv.at[me], qkv_out, qkv_sem, r, h)

    first = (z // 4 + yy) % 2
    own_rows = pl.multiple_of((yb * 2 + c) * NROWS, 16)
    near_rows = pl.multiple_of(((1 - yb) * 2 + c) * NROWS, 16)

    def spread(src, rows, size, send, recv):
        def one(k, carry):
            zd = first + 2 * k
            dst = b_buf.at[z % 4, pl.ds(rows, size)]

            @pl.when(zd == z)
            def _():
                pltpu.make_async_copy(src, dst, recv).start()

            @pl.when(zd != z)
            def _():
                remote(src, dst, send, recv, at(z_=zd)).start()

            return carry

        lax.fori_loop(0, 4, one, 0)

    remote(
        w_own.at[pl.ds(ZROWS, YROWS)], near, near_out, near_sem, at(yl_=2 * yy + 1 - yb)
    ).start()
    spread(w_own, own_rows, NROWS, b_out, b_sem)

    loads[3].wait()

    def temporal(r, carry):
        for h in range(3):
            lanes = slice(h * HD, (h + 1) * HD)
            q = emb[r * 3 + h, 0].astype(F32)
            own_k = emb[r * 3 + h, 1].astype(F32)
            own_v = emb[r * 3 + h, 2].astype(F32)
            keys = cache[0, :, r, :, lanes].astype(F32)
            s = jnp.sum(q[None] * keys, axis=-1, keepdims=True) * SCALE
            own = jnp.sum(q * own_k, axis=-1, keepdims=True) * SCALE
            peak = jnp.maximum(jnp.max(s, axis=0), own)
            e = jnp.exp(s - peak[None])
            own_e = jnp.exp(own - peak)
            total = jnp.sum(e, axis=0) + own_e
            weights = e.astype(BF16).astype(F32)
            values = cache[1, :, r, :, lanes].astype(F32)
            summed = jnp.sum(weights * values, axis=0)
            summed = summed + own_e.astype(BF16).astype(F32) * own_v
            t_send[r * 3 + h] = (summed / total).astype(BF16)
        return carry

    lax.fori_loop(0, ROLL, temporal, 0)

    for r in range(ROLL):
        for h in range(3):
            to_attending(t_send.at[r * 3 + h], t_recv.at[me], t_out, t_sem, r, h)

    await_bytes(near, near_sem)
    spread(near, near_rows + ZROWS, YROWS, bz_out, bz_sem)

    @pl.when(attends)
    def _():
        await_bytes(qkv, qkv_sem)
        remote(qkv.at[:, pl.ds(1, 2)], kv_peer, kv_out, kv_sem, at(c_=1 - c)).start()

    await_bytes(b_buf.at[:, pl.ds(own_rows, NROWS)], b_sem)
    went = b_buf.at[:, pl.ds(own_rows, ZROWS)]
    remote(went, went, by_out, by_sem, at(yl_=2 * yy + 1 - yb)).start()
    gathered = b_buf.at[:, pl.ds(own_rows, NROWS)]
    remote(gathered, gathered, bc_out, bc_sem, at(c_=1 - c)).start()

    @pl.when(attends)
    def _():
        await_bytes(kv_peer, kv_sem)
        await_bytes(t_recv, t_sem)
        c2 = SCALE * LOG2E

        def attend(i, carry):
            q = qkv[pl.ds(i * 8, 8), 0].reshape(128, HD)
            s_a = nt_dot(q, qkv[:, 1].reshape(512, HD))
            s_b = nt_dot(q, kv_peer[:, 0].reshape(512, HD))
            peak = jnp.maximum(
                jnp.max(s_a, axis=-1, keepdims=True), jnp.max(s_b, axis=-1, keepdims=True)
            )
            e_a = jnp.exp2((s_a - peak) * c2)
            e_b = jnp.exp2((s_b - peak) * c2)
            total = jnp.sum(e_a, axis=-1, keepdims=True) + jnp.sum(e_b, axis=-1, keepdims=True)
            o = jnp.dot(
                e_a.astype(BF16), qkv[:, 2].reshape(512, HD), preferred_element_type=F32
            ) + jnp.dot(
                e_b.astype(BF16), kv_peer[:, 1].reshape(512, HD), preferred_element_type=F32
            )
            o = o / total + t_recv[pl.ds(i * 8, 8)].astype(F32).reshape(128, HD)
            o_buf[i] = o.astype(BF16).reshape(2, 2, 2, 16, HD)
            for b in range(2):
                for step in (2, 1, 3, 0):
                    yd = (yl + step) % 4
                    zd = 2 * i + b
                    here = jnp.logical_and(zd == z, yl == yd)
                    src, dst = o_buf.at[i, :, :, (yl + step) % 2], att.at[pair_head, :, :, pair_roll]

                    @pl.when(here)
                    def _(src=src, dst=dst):
                        pltpu.make_async_copy(src, dst, o_sem.at[pair_roll // 2]).start()

                    @pl.when(jnp.logical_not(here))
                    def _(src=src, dst=dst, zd=zd, yd=yd):
                        remote(
                            src, dst, o_out.at[i], o_sem.at[pair_roll // 2], at(z_=zd, yl_=yd)
                        ).start()

            return carry

        lax.fori_loop(0, 4, attend, 0)

    await_bytes(b_buf.at[:, pl.ds(near_rows, ZROWS)], by_sem)
    await_bytes(b_buf.at[:, pl.ds(near_rows, YROWS)], bz_sem)
    gathered_near = b_buf.at[:, pl.ds(near_rows, NROWS)]
    remote(gathered_near, gathered_near, bd_out, bd_sem, at(c_=1 - c)).start()

    await_bytes(b_buf.at[:, pl.ds(own_rows, NROWS)], bc_sem)
    await_bytes(b_buf.at[:, pl.ds(near_rows, NROWS)], bd_sem)
    blank = jnp.zeros((64, 384), BF16)
    main_rows = pl.multiple_of(yy * 64, 64)
    tail_rows = pl.multiple_of((1 - yy) * 256, 64)
    mine = yh == half
    early = jnp.where(mine, 1 - yy, yy)
    order = (early, 1 - early)
    spans = [pl.ds(pl.multiple_of(order[i] * 32, 32), 32) for i in range(2)]

    for w in range(2):
        await_bytes(att.at[:, :, :, pl.ds(2 * w, 2)], o_sem.at[w])
        tokens = [
            jnp.concatenate(
                [att[h, zz, :, 2 * w : 2 * w + 2].reshape(64, HD) for h in range(3)], axis=1
            )
            for zz in range(2)
        ]
        stacked = jnp.concatenate(tokens, axis=0)
        beside = jnp.concatenate(tokens, axis=1)

        def project(xd, stacked=stacked, beside=beside):
            main = nt_dot(stacked, b_buf[xd, pl.ds(main_rows, 256), :])
            ends = b_buf[xd, pl.ds(tail_rows, 64), :]
            weights = jnp.concatenate(
                [
                    jnp.concatenate([ends, blank], axis=1),
                    jnp.concatenate([blank, ends], axis=1),
                ],
                axis=0,
            )
            return jnp.concatenate([main[:64], main[64:], nt_dot(beside, weights)], axis=1)

        def to_x(i, n, k, w=w):
            remote(
                cx_send.at[w, n, spans[i]], cx_recv.at[w, i, n], cx_out, cx_sem.at[2 * w + i],
                at(x_=(x + k) % 4),
            ).start()

        for n, k in enumerate((2, 3, 1)):
            cx_send[w, n] = project((x + k) % 4).astype(BF16)
            to_x(0, n, k)
        for n, k in enumerate((2, 3, 1)):
            to_x(1, n, k)
        cx_own[w] = project(x)

    lane_half = lax.broadcasted_iota(jnp.int32, (32, 128), 1) // 64
    main_lanes = pl.multiple_of(yy * 128, 128)
    tail_lanes = pl.multiple_of((1 - yy) * 256, 128)
    for w in range(2):
        for i in range(2):
            await_bytes(cx_recv.at[w, i], cx_sem.at[2 * w + i])
            total = cx_own[w, spans[i]]
            for n in range(3):
                total = total + cx_recv[w, i, n].astype(F32)
            ends = total[:, 512:640]
            turned = pltpu.roll(ends, 64, 1)
            for zz in range(2):
                placed = jnp.where(lane_half == yy, jnp.where(yy == zz, ends, turned), 0.0)
                y_send[w, i, zz, :, pl.ds(main_lanes, 256)] = total[
                    :, zz * 256 : zz * 256 + 256
                ].astype(BF16)
                y_send[w, i, zz, :, pl.ds(tail_lanes, 128)] = placed.astype(BF16)
                src, dst = y_send.at[w, i, zz], y_out_ref.at[yh, yy, w]
                here = jnp.logical_and(mine, jnp.logical_and(z % 2 == zz, order[i] == yy))

                @pl.when(here)
                def _(src=src, dst=dst):
                    pltpu.make_async_copy(src, dst, y_sem).start()

                @pl.when(jnp.logical_not(here))
                def _(src=src, dst=dst, zz=zz, i=i):
                    remote(
                        src, dst, y_out, y_sem, at(z_=base + zz, yl_=2 * order[i] + yb, yh_=half)
                    ).start()

    await_bytes(y_out_ref, y_sem)

    @pl.when(mine)
    def _():
        await_bytes(b_buf.at[0, pl.ds(0, 192)], y_out)

    @pl.when(jnp.logical_not(mine))
    def _():
        await_bytes(y_out_ref, y_out)

    @pl.when(attends)
    def _():
        await_bytes(emb.at[pl.ds(0, 11)], qkv_out)
        await_bytes(t_send.at[pl.ds(0, 11)], t_out)
        await_bytes(kv_peer, kv_out)
        for i in range(4):

            @pl.when(z // 2 == i)
            def _(i=i):
                await_bytes(kv_peer.at[pl.ds(0, 14)], o_out.at[i])

            @pl.when(z // 2 != i)
            def _(i=i):
                await_bytes(kv_peer.at[pl.ds(0, 16)], o_out.at[i])

    @pl.when(jnp.logical_not(attends))
    def _():
        await_bytes(emb, qkv_out)
        await_bytes(t_send, t_out)

    @pl.when(z % 2 == first)
    def _():
        await_bytes(b_buf.at[pl.ds(0, 3), pl.ds(0, NROWS)], b_out)
        await_bytes(b_buf.at[pl.ds(0, 3), pl.ds(0, YROWS)], bz_out)

    @pl.when(z % 2 != first)
    def _():
        await_bytes(b_buf.at[:, pl.ds(0, NROWS)], b_out)
        await_bytes(b_buf.at[:, pl.ds(0, YROWS)], bz_out)

    await_bytes(near, near_out)
    await_bytes(b_buf.at[:, pl.ds(0, ZROWS)], by_out)
    await_bytes(b_buf.at[:, pl.ds(0, NROWS)], bc_out)
    await_bytes(b_buf.at[:, pl.ds(0, NROWS)], bd_out)
    await_bytes(cx_send, cx_out)


def shards(fresh, still_masked, actions, action_table, mask_vector, position, cache, w_out):
    anywhere = pl.BlockSpec(memory_space=pl.ANY)
    vmem = pl.BlockSpec(memory_space=pltpu.VMEM)
    smem = pl.BlockSpec(memory_space=pltpu.SMEM)
    dma = pltpu.SemaphoreType.DMA
    parts = pl.pallas_call(
        kernel,
        out_shape=jax.ShapeDtypeStruct((2, 2, 2, 32, 384), BF16),
        in_specs=[smem, vmem, vmem, vmem, anywhere, anywhere, anywhere, anywhere],
        out_specs=anywhere,
        scratch_shapes=[
            pltpu.VMEM((3, 4, 16, 384), BF16),
            pltpu.VMEM((3, 16, 384), BF16),
            pltpu.VMEM((2, 16, 4, 16, 384), BF16),
            pltpu.VMEM((NROWS, 384), BF16),
            pltpu.VMEM((12, 3, 16, HD), BF16),
            pltpu.VMEM((32, 3, 16, HD), BF16),
            pltpu.VMEM((32, 2, 16, HD), BF16),
            pltpu.VMEM((12, 16, HD), BF16),
            pltpu.VMEM((32, 16, HD), BF16),
            pltpu.VMEM((4, 2, 2, 2, 16, HD), BF16),
            pltpu.VMEM((3, 2, 2, 4, 16, HD), BF16),
            pltpu.VMEM((YROWS, 384), BF16),
            pltpu.VMEM((4, 4 * NROWS, 384), BF16),
            pltpu.VMEM((2, 3, 64, 640), BF16),
            pltpu.VMEM((2, 64, 640), F32),
            pltpu.VMEM((2, 2, 3, 32, 640), BF16),
            pltpu.VMEM((2, 2, 2, 32, 384), BF16),
            dma((4,)),
            dma((4,)),
            dma((4,)),
            dma((2,)),
        ]
        + [dma] * 21,
        compiler_params=pltpu.CompilerParams(
            collective_id=0, has_side_effects=True, vmem_limit_bytes=60 << 20
        ),
        cost_estimate=pl.CostEstimate(
            flops=400_000_000, bytes_accessed=2_000_000, transcendentals=600_000
        ),
    )(
        actions,
        still_masked,
        jnp.transpose(action_table, (1, 0, 2)),
        mask_vector,
        fresh,
        position,
        cache,
        jnp.transpose(w_out),
    )
    parts = parts.reshape(2, 2, 64, 384)
    return sum(
        jnp.pad(parts[k, b].astype(F32), ((0, 0), (256 * b, 256 * (1 - b))))
        for k in range(2)
        for b in range(2)
    ).reshape(4, 16, 640)


def solution(mesh):
    placed = (
        P(None, None, "patch", "head"),
        P(None, "patch"),
        P(),
        P(None, None, "head"),
        P(None, "head"),
        P(None, "patch", "head"),
        P(None, None, None, "patch", "head"),
        P("head", "patch"),
    )
    return jax.shard_map(
        shards, mesh=mesh, in_specs=placed, out_specs=P(None, "patch", "head"), check_vma=False
    )
```
